256 devices in a mesh: row: 8 (over y_lo, x), col: 32 (over y_hi, z, core).
Axes of the slice: x: 4, y: 4 (y_hi: 2, y_lo: 2; y = y_hi * 2 + y_lo), z: 8, core: 2. Of those that a mesh axis runs over, the one named last changes fastest.
Arguments:
- inputs: bfloat16 [256, 14336], P('col', 'row'), may hold values from -6 to 6
- out_grad: bfloat16 [256, 14336], P('col', 'row'), may hold values from -6 to 6
- w_in: bfloat16 [14336, 29696], P('row', 'col'), may hold values from -0.046875 to 0.046875
- w_out: bfloat16 [29696, 14336], P('col', 'row'), may hold values from -0.03125 to 0.03125
Outputs:
- in_grad: bfloat16 [256, 14336], P('col', 'row')
- w_in_grad: bfloat16 [14336, 29696], P('row', 'col')
- w_out_grad: bfloat16 [29696, 14336], P('col', 'row')
The draws below stay inside these ranges and needn't reach their ends.
All inputs are finite; a program needn't handle non-finite values.
Results may differ from the reference program's by a relative error of at most 0.022.
Values may be sent and summed in bfloat16 or wider, within the bound.
A program may use at most 64 MiB of HBM per device.

```python
import math
import jax
import jax.numpy as jnp
from jax import lax

D = 14336
FF = 29696
TOKENS = 256


def steps_of(own_key, shape, shards, smallest, top_value):
    def one(axis_at, blocks):
        steps = jax.random.uniform(jax.random.fold_in(jax.random.fold_in(own_key, 6), axis_at), (blocks,), jnp.float32, smallest / len(shards), top_value / len(shards))
        return jnp.repeat(jnp.exp(steps), shape[axis_at] // blocks).reshape((-1,) + (1,) * (len(shape) - axis_at - 1))

    level = one(*shards[0])
    for cut in shards[1:]:
        level = level * one(*cut)
    return level


def normal_values(own_key, shape, scale, bound, shards=(), dtype=jnp.bfloat16):
    factor_of = steps_of(own_key, shape, shards, -0.22, 0.18) if shards else 1.0
    array = jax.random.normal(own_key, shape, jnp.float32) * scale * factor_of
    return jnp.minimum(jnp.maximum(array, -bound), bound).astype(dtype)


def setup_inputs(seed: int = 0) -> dict:
    key_of = jax.random.split(jax.random.key(seed), 5)
    return {
        "inputs": normal_values(key_of[0], (TOKENS, D), 1.0, 6.0, ((0, 32), (1, 8))),
        "out_grad": normal_values(key_of[1], (TOKENS, D), 1.0, 6.0, ((0, 32), (1, 8))),
        "w_in": normal_values(key_of[2], (D, FF), D ** -0.5, 0.046875, ((0, 8), (1, 32))),
        "w_out": normal_values(key_of[3], (FF, D), FF ** -0.5, 0.03125, ((0, 32), (1, 8))),
    }


def reference(inputs, out_grad, w_in, w_out):
    pre = jnp.dot(inputs, w_in, preferred_element_type=jnp.float32)
    back = lax.dot_general(out_grad, w_out, (((1,), (1,)), ((), ())), preferred_element_type=jnp.float32)
    cdf = 0.5 * (1.0 + jax.scipy.special.erf(pre / math.sqrt(2.0)))
    hidden = (pre * cdf).astype(jnp.bfloat16)
    slope = cdf + pre * jnp.exp(-0.5 * pre * pre) / math.sqrt(2.0 * math.pi)
    pre_grad = (back * slope).astype(jnp.bfloat16)
    w_out_grad = lax.dot_general(hidden, out_grad, (((0,), (0,)), ((), ())), preferred_element_type=jnp.float32).astype(jnp.bfloat16)
    w_in_grad = lax.dot_general(inputs, pre_grad, (((0,), (0,)), ((), ())), preferred_element_type=jnp.float32).astype(jnp.bfloat16)
    in_grad = lax.dot_general(pre_grad, w_in, (((1,), (1,)), ((), ())), preferred_element_type=jnp.float32).astype(jnp.bfloat16)
    return (in_grad, w_in_grad, w_out_grad)
```

```python
import functools
import math

import jax
import jax.numpy as jnp
from jax import lax
from jax.experimental import pallas as pl
from jax.experimental.pallas import tpu as pltpu
from jax.sharding import PartitionSpec as P

MESH = pl.DeviceIdType.MESH
BF16, F32 = jnp.bfloat16, jnp.float32
NT = (((1,), (1,)), ((), ()))
NN = (((1,), (0,)), ((), ()))
TN = (((0,), (0,)), ((), ()))

T = 8
D = 1792
HALF = D // 2
F = 928
ROWS = 8

BLOCKS = (
    (0, 0), (0, 1), (0, -1), (1, 0),
    (0, 2), (0, -2), (1, 1), (1, -1),
    (0, 3), (0, -3), (1, 2), (1, -2),
    (0, 4), (1, 3), (1, -3), (1, 4),
)
SLOT = {block: i for i, block in enumerate(BLOCKS)}
BATCHES = 4
PER = len(BLOCKS) // BATCHES
TB = PER * 2 * T


def dot(a, b, dims):
    return lax.dot_general(a, b, dims, preferred_element_type=F32)


def mirrored(block):
    y, d = block
    return SLOT[(y, d if d == 4 else -d)]


def stack(a, b):
    return jnp.concatenate([a, b], axis=0)


def fetch_wait(ref, sem):
    pltpu.make_async_copy(ref, ref, sem).wait()


def kernel(
    x_in_hbm, x_og_hbm, w_in_hbm, w_out_hbm,
    in_grad, w_in_grad, w_out_grad,
    x, w_in, w_out, mine, sibs, acts, part, part_in, act, hid, pgr, to_sib, keep, from_sib, comb, comb_in,
    x_sem, w_sem, mine_sem, sibs_sem, part_sem, act_sem, fs_sem, comb_sem,
    mine_out, sibs_out, part_out, act_out, fs_out, comb_out,
):
    r, c = lax.axis_index("row"), lax.axis_index("col")
    y_hi, z, k = c // 16, lax.rem(c // 2, 8), lax.rem(c, 2)

    def chip(y, d):
        return (r, lax.rem(y_hi + y, 2) * 16 + lax.rem(z + d + 8, 8) * 2 + k)

    sibling = (r, c + 1 - 2 * k)

    def peer(j):
        return lax.rem(r + j, ROWS)

    def send(src, dst, out, sem, to):
        pltpu.make_async_remote_copy(
            src_ref=src, dst_ref=dst, send_sem=out, recv_sem=sem, device_id=to, device_id_type=MESH
        ).start()

    weights = [pltpu.make_async_copy(w_in_hbm, w_in, w_sem.at[0]), pltpu.make_async_copy(w_out_hbm, w_out, w_sem.at[1])]
    tokens = [pltpu.make_async_copy(x_in_hbm, x.at[0], x_sem.at[0]), pltpu.make_async_copy(x_og_hbm, x.at[1], x_sem.at[1])]
    for copy in tokens + weights:
        copy.start()

    barrier = pltpu.get_barrier_semaphore()
    friends = [chip(*block) for block in BLOCKS[1:]] + [sibling] + [(peer(j), c) for j in range(1, ROWS)]
    for friend in friends:
        pl.semaphore_signal(barrier, inc=1, device_id=friend, device_id_type=MESH)
    for a in range(2):
        tokens[a].wait()
        block = x[a].astype(F32)
        mine[0, a] = stack(block[:, :HALF], block[:, HALF:]).astype(BF16)
    pl.semaphore_wait(barrier, len(friends))

    def hop(block, onward, to):
        slot = SLOT[onward]
        send(mine.at[SLOT[block]], mine.at[slot], mine_out, mine_sem.at[slot], to)

    def share(block):
        slot = SLOT[block]
        send(mine.at[slot], sibs.at[slot], sibs_out, sibs_sem.at[slot // PER], sibling)

    def forward(block):
        y, d = block
        if block == (0, 0):
            hop(block, (1, 0), chip(1, 0))
        if 0 <= d < 3 or block == (0, 3):
            hop(block, (y, d + 1), chip(0, -1))
        if -3 < d <= 0 or block == (1, -3):
            hop(block, (y, 4 if d == -3 else d - 1), chip(0, 1))
        share(block)

    def arrive(block):
        slot = SLOT[block]
        fetch_wait(mine.at[slot], mine_sem.at[slot])
        forward(block)

    def up(b):
        fetch_wait(sibs.at[pl.ds(PER * b, PER)], sibs_sem.at[b])
        for s in range(PER * b, PER * b + PER):
            for a in range(2):
                own, sib = mine[s, a], sibs[s, a]
                acts[a, 16 * s : 16 * s + 16, :HALF] = stack(own[:T], sib[:T])
                acts[a, 16 * s : 16 * s + 16, HALF:] = stack(own[T:], sib[T:])
        rows = slice(TB * b, TB * b + TB)
        pre = dot(acts[0, rows], w_in[...], NT)
        back = dot(acts[1, rows], w_out[...], NT)
        for i in range(ROWS):
            part[b, i] = stack(pre[T * i : T * i + T], back[T * i : T * i + T]).astype(BF16)
        for j in range(1, ROWS):
            send(part.at[b, peer(j)], part_in.at[b, j - 1], part_out.at[b], part_sem.at[b], (peer(j), c))

    def activate(b):
        fetch_wait(part_in.at[b], part_sem.at[b])
        total = part[b, r].astype(F32)
        for j in range(ROWS - 1):
            total += part_in[b, j].astype(F32)
        pre, back = total[:T], total[T:]
        cdf = 0.5 * (1.0 + lax.erf(pre * (1.0 / math.sqrt(2.0))))
        slope = cdf + pre * jnp.exp(-0.5 * pre * pre) * (1.0 / math.sqrt(2.0 * math.pi))
        act[b, r] = stack(pre * cdf, back * slope).astype(BF16)
        for j in range(1, ROWS):
            send(act.at[b, r], act.at[b, r], act_out.at[b], act_sem.at[b], (peer(j), c))

    def down(b):
        fetch_wait(act.at[b, pl.ds(0, ROWS - 1)], act_sem.at[b])
        for i in range(0, ROWS, 2):
            one, two = act[b, i], act[b, i + 1]
            at = TB * b + T * i
            hid[at : at + 16] = stack(one[:T], two[:T])
            pgr[at : at + 16] = stack(one[T:], two[T:])
        grad = dot(pgr[TB * b : TB * b + TB], w_in[...], NN)
        for i in range(PER):
            own, sib = grad[16 * i : 16 * i + T], grad[16 * i + T : 16 * i + 16]
            to_sib[b, i] = stack(sib[:, :HALF], sib[:, HALF:]).astype(BF16)
            keep[b, i] = stack(own[:, :HALF], own[:, HALF:])
        send(to_sib.at[b], from_sib.at[b], fs_out.at[b], fs_sem.at[b], sibling)

    def combine(b):
        fetch_wait(from_sib.at[b], fs_sem.at[b])
        for i in range(PER):
            s = PER * b + i
            total = keep[b, i] + from_sib[b, i].astype(F32)
            if s == 0:
                keep[0, 0] = total
            else:
                comb[s] = total.astype(BF16)
                send(comb.at[s], comb_in.at[mirrored(BLOCKS[s])], comb_out.at[b], comb_sem.at[b], chip(*BLOCKS[s]))

    forward((0, 0))
    for block in ((0, 1), (0, -1), (1, 0)):
        arrive(block)
    for copy in weights:
        copy.wait()
    for block in ((0, 2), (0, -2), (1, 1), (1, -1)):
        arrive(block)
    up(0)
    for block in ((0, 3), (0, -3), (1, 2), (1, -2)):
        arrive(block)
    up(1)
    activate(0)
    for block in ((0, 4), (1, 3), (1, -3)):
        arrive(block)
    up(2)
    activate(1)
    arrive((1, 4))
    down(0)
    up(3)
    activate(2)
    down(1)
    combine(0)
    activate(3)
    down(2)
    combine(1)
    down(3)
    combine(2)
    combine(3)
    w_out_grad[...] = dot(hid[...], acts[1], TN).astype(BF16)
    w_in_grad[...] = dot(pgr[...], acts[0], TN).astype(BF16)
    total = keep[0, 0]
    for b in range(BATCHES):
        low = max(PER * b, 1)
        fetch_wait(comb_in.at[pl.ds(low, PER * (b + 1) - low)], comb_sem.at[b])
        for s in range(low, PER * (b + 1)):
            total += comb_in[s].astype(F32)
    in_grad[:, :HALF] = total[:T].astype(BF16)
    in_grad[:, HALF:] = total[T:].astype(BF16)

    fetch_wait(mine.at[pl.ds(1, len(BLOCKS) - 1)], mine_out)
    fetch_wait(sibs, sibs_out)
    for b in range(BATCHES):
        low = max(PER * b, 1)
        fetch_wait(part_in.at[b], part_out.at[b])
        fetch_wait(act.at[b, pl.ds(0, ROWS - 1)], act_out.at[b])
        fetch_wait(to_sib.at[b], fs_out.at[b])
        fetch_wait(comb.at[pl.ds(low, PER * (b + 1) - low)], comb_out.at[b])


PIECES = 2


def flush(x, gi, go, x_hbm, gi_hbm, go_hbm, sem):
    copies = [pltpu.make_async_copy(x, x_hbm, sem.at[2 * PIECES])]
    n = F // PIECES
    for i in range(PIECES):
        at = pl.ds(n * i, n)
        copies.append(pltpu.make_async_copy(gi.at[at], gi_hbm.at[at], sem.at[2 * i]))
        copies.append(pltpu.make_async_copy(go.at[at], go_hbm.at[at], sem.at[2 * i + 1]))
    for copy in copies:
        copy.start()
    for copy in copies:
        copy.wait()


def on_device(inputs, out_grad, w_in, w_out):
    vmem = pl.BlockSpec(memory_space=pltpu.VMEM)
    hbm = pl.BlockSpec(memory_space=pl.ANY)
    n = len(BLOCKS)
    dma = pltpu.SemaphoreType.DMA
    outs = pl.pallas_call(
        kernel,
        out_shape=(pltpu.VMEM((T, D), BF16), pltpu.VMEM((F, D), BF16), pltpu.VMEM((F, D), BF16)),
        in_specs=[hbm] * 4,
        out_specs=(vmem, vmem, vmem),
        scratch_shapes=[
            pltpu.VMEM((2, T, D), BF16),
            pltpu.VMEM((F, D), BF16),
            pltpu.VMEM((F, D), BF16),
            pltpu.VMEM((n, 2, 16, HALF), BF16),
            pltpu.VMEM((n, 2, 16, HALF), BF16),
            pltpu.VMEM((2, 16 * n, D), BF16),
            pltpu.VMEM((BATCHES, ROWS, 16, F), BF16),
            pltpu.VMEM((BATCHES, ROWS - 1, 16, F), BF16),
            pltpu.VMEM((BATCHES, ROWS, 16, F), BF16),
            pltpu.VMEM((16 * n, F), BF16),
            pltpu.VMEM((16 * n, F), BF16),
            pltpu.VMEM((BATCHES, PER, 16, HALF), BF16),
            pltpu.VMEM((BATCHES, PER, 16, HALF), F32),
            pltpu.VMEM((BATCHES, PER, 16, HALF), BF16),
            pltpu.VMEM((n, 16, HALF), BF16),
            pltpu.VMEM((n, 16, HALF), BF16),
            dma((2,)),
            dma((2,)),
            dma((n,)),
            dma((BATCHES,)),
            dma((BATCHES,)),
            dma((BATCHES,)),
            dma((BATCHES,)),
            dma((BATCHES,)),
            dma,
            dma,
            dma((BATCHES,)),
            dma((BATCHES,)),
            dma((BATCHES,)),
            dma((BATCHES,)),
        ],
        compiler_params=pltpu.CompilerParams(collective_id=0, has_side_effects=True, vmem_limit_bytes=44 << 20),
        name="block",
    )(*(pltpu.with_memory_space_constraint(a, pltpu.HBM) for a in (inputs, out_grad, w_in.T, w_out)))
    in_grad, w_in_grad, w_out_grad = pl.pallas_call(
        flush,
        out_shape=tuple(jax.ShapeDtypeStruct(o.shape, BF16) for o in outs),
        in_specs=[vmem] * 3,
        out_specs=(hbm,) * 3,
        scratch_shapes=[dma((2 * PIECES + 1,))],
        compiler_params=pltpu.CompilerParams(vmem_limit_bytes=16 << 20),
        name="flush",
    )(*outs)
    return (in_grad, w_in_grad.T, w_out_grad)


def solution(mesh):
    placed = (P("col", "row"), P("col", "row"), P("row", "col"), P("col", "row"))
    return jax.shard_map(
        on_device,
        mesh=mesh,
        in_specs=placed,
        out_specs=(P("col", "row"), P("row", "col"), P("col", "row")),
        check_vma=False,
    )
```

```python
import functools
import math

import jax
import jax.numpy as jnp
from jax import lax
from jax.experimental import pallas as pl
from jax.experimental.pallas import tpu as pltpu
from jax.sharding import PartitionSpec as P

MESH = pl.DeviceIdType.MESH
BF16, F32 = jnp.bfloat16, jnp.float32
NT = (((1,), (1,)), ((), ()))
NN = (((1,), (0,)), ((), ()))
TN = (((0,), (0,)), ((), ()))

T = 8
D = 1792
HALF = D // 2
F = 928
WIDE = 512
ROWS = 8

BLOCKS = (
    (0, 1), (0, -1), (1, 0), (0, 2),
    (0, -2), (1, 1), (1, -1), (0, 3),
    (0, -3), (1, 2), (1, -2), (0, 4),
    (1, 3), (1, -3), (1, 4), (0, 0),
)
ONWARD = {
    (0, 0): ((0, 2), (0, -2), (1, 0), (0, 1), (0, -1)),
    (0, 1): ((1, 0),),
    (0, -1): ((1, 0),),
    (0, 2): ((0, -1), (1, 0)),
    (0, -2): ((0, 1), (1, 0)),
    (0, 4): ((1, 0),),
    (1, 2): ((0, -1),),
    (1, -2): ((0, 1),),
}
SLOT = {block: i for i, block in enumerate(BLOCKS)}
HOME = SLOT[(0, 0)]
BATCHES = 4
PER = len(BLOCKS) // BATCHES
TB = PER * 2 * T


SUM_DIRECT = (2, 3)
SPREAD_DIRECT = (0, 1, 2, 3)


def dot(a, b, dims):
    return lax.dot_general(a, b, dims, preferred_element_type=F32)


def mirrored(block):
    y, d = block
    return SLOT[(y, d if d == 4 else -d)]


def stack(a, b):
    return jnp.concatenate([a, b], axis=0)


def folded(x):
    pad = jnp.zeros((T, 2 * WIDE - F), F32)
    return stack(x[:, :WIDE], jnp.concatenate([x[:, WIDE:], pad], axis=1)).astype(BF16)


def unfold(ref, at, one, two):
    ref[at : at + 16, :WIDE] = stack(one[:T], two[:T])
    ref[at : at + 16, WIDE:] = stack(one[T:, : F - WIDE], two[T:, : F - WIDE])


def fetch_wait(ref, sem):
    pltpu.make_async_copy(ref, ref, sem).wait()


def kernel(
    x_in_hbm, x_og_hbm, w_in_hbm, w_out_hbm,
    in_grad, w_in_grad, w_out_grad,
    x, w_in, w_out, w_in_t, w_out_t, mine, sibs, acts, part, part_in, x_in, y_to, y_in, own_row, act, late, hid, pgr, to_sib, keep, from_sib, comb, comb_in,
    x_sem, w_sem, mine_sem, sibs_sem, part_sem, y_sem, act_sem, act_y_sem, late_sem, late_y_sem, fs_sem, comb_sem,
    mine_out, sibs_out, part_out, y_out, act_out, late_out, fs_out, comb_out,
):
    r, c = lax.axis_index("row"), lax.axis_index("col")
    y_hi, z, k = c // 16, lax.rem(c // 2, 8), lax.rem(c, 2)

    def chip(y, d):
        return (r, lax.rem(y_hi + y, 2) * 16 + lax.rem(z + d + 8, 8) * 2 + k)

    sibling = (r, c + 1 - 2 * k)

    y_lo, x_at = r // 4, lax.rem(r, 4)
    me = 2 * x_at + y_lo
    y_peer = (lax.rem(r + 4, ROWS), c)

    def peer(j):
        return lax.rem(r + j, ROWS)

    def x_peer(j):
        return (4 * y_lo + lax.rem(x_at + j, 4), c)

    def send(src, dst, out, sem, to):
        pltpu.make_async_remote_copy(
            src_ref=src, dst_ref=dst, send_sem=out, recv_sem=sem, device_id=to, device_id_type=MESH
        ).start()

    weights = [pltpu.make_async_copy(w_in_hbm, w_in, w_sem.at[0]), pltpu.make_async_copy(w_out_hbm, w_out, w_sem.at[1])]
    tokens = [pltpu.make_async_copy(x_in_hbm, x.at[0], x_sem.at[0]), pltpu.make_async_copy(x_og_hbm, x.at[1], x_sem.at[1])]
    for copy in tokens + weights:
        copy.start()

    barrier = pltpu.get_barrier_semaphore()
    friends = [chip(*block) for block in ONWARD[(0, 0)]] + [sibling] + [(peer(j), c) for j in range(1, ROWS)]
    for friend in friends:
        pl.semaphore_signal(barrier, inc=1, device_id=friend, device_id_type=MESH)
    for a in range(2):
        tokens[a].wait()
        block = x[a].astype(F32)
        mine[HOME, a] = stack(block[:, :HALF], block[:, HALF:]).astype(BF16)
    pl.semaphore_wait(barrier, len(friends))

    def forward(block):
        slot = SLOT[block]
        for to in ONWARD.get(block, ()):
            seen = SLOT[((block[0] + to[0]) % 2, block[1] - to[1])]
            send(mine.at[slot], mine.at[seen], mine_out, mine_sem.at[seen], chip(*to))
        if block == (0, -2):
            far, near = SLOT[(0, 4)], SLOT[(0, 2)]
            send(mine.at[near + k * (slot - near)], mine.at[far], mine_out, mine_sem.at[far], chip(0, 4 * k - 2))
        send(mine.at[slot], sibs.at[slot], sibs_out, sibs_sem.at[slot], sibling)

    def arrive(*blocks):
        for block in blocks:
            slot = SLOT[block]
            fetch_wait(mine.at[slot], mine_sem.at[slot])
            forward(block)

    sums = {}

    def up_in(b):
        for s in range(PER * b, PER * b + PER):
            fetch_wait(sibs.at[s], sibs_sem.at[s])
            for a in range(2):
                own, sib = mine[s, a], sibs[s, a]
                acts[a, 16 * s : 16 * s + 16, :HALF] = stack(own[:T], sib[:T])
                acts[a, 16 * s : 16 * s + 16, HALF:] = stack(own[T:], sib[T:])
        sums[b] = dot(acts[0, TB * b : TB * b + TB], w_in_t[...], NN)

    def up_og(b):
        pre, back = sums[b], dot(acts[1, TB * b : TB * b + TB], w_out_t[...], NN)
        for i in range(ROWS):
            part[b, i // 2, i % 2] = stack(pre[T * i : T * i + T], back[T * i : T * i + T]).astype(BF16)
        if b in SUM_DIRECT:
            for j in range(1, ROWS):
                to = peer(j)
                send(part.at[b, lax.rem(to, 4), to // 4], part_in.at[b, j - 1], part_out.at[b], part_sem.at[b], (to, c))
        else:
            for j in range(1, 4):
                send(part.at[b, lax.rem(x_at + j, 4)], x_in.at[b, j - 1], part_out.at[b], part_sem.at[b], x_peer(j))

    def along_x(b):
        if b in SUM_DIRECT:
            return
        fetch_wait(x_in.at[b], part_sem.at[b])

        def over_x(lane):
            total = part[b, x_at, lane].astype(F32)
            for j in range(3):
                total += x_in[b, j, lane].astype(F32)
            return total

        y_to[b] = over_x(1 - y_lo).astype(BF16)
        send(y_to.at[b], y_in.at[b], y_out.at[b], y_sem.at[b], y_peer)
        own_row[b] = over_x(y_lo)

    def activate(b):
        if b in SUM_DIRECT:
            fetch_wait(part_in.at[b], part_sem.at[b])
            total = part[b, x_at, y_lo].astype(F32)
            for j in range(ROWS - 1):
                total += part_in[b, j].astype(F32)
        else:
            fetch_wait(y_in.at[b], y_sem.at[b])
            total = own_row[b] + y_in[b].astype(F32)
        pre, back = total[:T], total[T:]
        cdf = 0.5 * (1.0 + lax.erf(pre * (1.0 / math.sqrt(2.0))))
        slope = cdf + pre * jnp.exp(-0.5 * pre * pre) * (1.0 / math.sqrt(2.0 * math.pi))
        act[b, me] = folded(back * slope)
        late[me, b] = folded(pre * cdf)
        own = act.at[b, me]
        if b in SPREAD_DIRECT:
            for j in range(1, ROWS):
                send(own, own, act_out.at[b], act_sem.at[b], (peer(j), c))
        else:
            send(own, own, act_out.at[b], act_y_sem.at[b], y_peer)
            for j in range(1, 4):
                send(own, own, act_out.at[b], act_sem.at[b], x_peer(j))

    def relay(b):
        if b in SPREAD_DIRECT:
            return
        other = act.at[b, 2 * x_at + 1 - y_lo]
        fetch_wait(other, act_y_sem.at[b])
        for j in range(1, 4):
            send(other, other, act_out.at[b], act_sem.at[b], x_peer(j))

    def spread_late():
        own = late.at[me]
        send(own, own, late_out, late_y_sem, y_peer)
        for j in range(1, 4):
            send(own, own, late_out, late_sem, x_peer(j))

    def relay_late():
        other = late.at[2 * x_at + 1 - y_lo]
        fetch_wait(other, late_y_sem)
        for j in range(1, 4):
            send(other, other, late_out, late_sem, x_peer(j))

    def down(b):
        fetch_wait(act.at[b, pl.ds(0, ROWS - (1 if b in SPREAD_DIRECT else 2))], act_sem.at[b])
        for i in range(0, ROWS, 2):
            unfold(pgr, TB * b + T * i, act[b, i], act[b, i + 1])
        grad = dot(pgr[TB * b : TB * b + TB], w_in[...], NN)
        for i in range(PER):
            own, sib = grad[16 * i : 16 * i + T], grad[16 * i + T : 16 * i + 16]
            to_sib[b, i] = stack(sib[:, :HALF], sib[:, HALF:]).astype(BF16)
            keep[b, i] = stack(own[:, :HALF], own[:, HALF:])
        send(to_sib.at[b], from_sib.at[b], fs_out.at[b], fs_sem.at[b], sibling)

    def combine(b):
        fetch_wait(from_sib.at[b], fs_sem.at[b])
        for i in range(PER):
            s = PER * b + i
            total = keep[b, i] + from_sib[b, i].astype(F32)
            if s == HOME:
                keep[b, i] = total
            else:
                comb[s] = total.astype(BF16)
                seen = mirrored(BLOCKS[s])
                send(comb.at[s], comb_in.at[seen], comb_out, comb_sem.at[seen], chip(*BLOCKS[s]))

    forward((0, 0))
    weights[0].wait()
    w_in_t[...] = w_in[...].T
    weights[1].wait()
    w_out_t[...] = w_out[...].T
    arrive((0, 2), (0, -2), (0, 1), (0, -1), (1, 0))
    up_in(0)
    up_og(0)
    arrive((1, 2), (1, -2), (0, 4), (1, 1), (1, -1), (0, 3), (0, -3))
    up_in(1)
    up_og(1)
    along_x(0)
    up_in(2)
    arrive((1, 3), (1, -3))
    up_og(2)
    activate(0)
    arrive((1, 4))
    up_in(3)
    along_x(1)
    up_og(3)
    activate(1)
    along_x(2)
    activate(2)
    down(0)
    combine(0)
    along_x(3)
    activate(3)
    spread_late()
    down(1)
    combine(1)
    down(2)
    combine(2)
    relay_late()
    down(3)
    combine(3)
    w_in_grad[...] = dot(pgr[...], acts[0], TN).astype(BF16)
    fetch_wait(late.at[pl.ds(0, ROWS - 2)], late_sem)
    for b in range(BATCHES):
        for i in range(0, ROWS, 2):
            unfold(hid, TB * b + T * i, late[i, b], late[i + 1, b])
    w_out_grad[...] = dot(hid[...], acts[1], TN).astype(BF16)
    total = keep[HOME // PER, HOME % PER]
    for s in range(len(BLOCKS)):
        if s == HOME:
            continue
        fetch_wait(comb_in.at[s], comb_sem.at[s])
        total += comb_in[s].astype(F32)
    in_grad[:, :HALF] = total[:T].astype(BF16)
    in_grad[:, HALF:] = total[T:].astype(BF16)

    fetch_wait(mine.at[pl.ds(0, len(BLOCKS) - 1)], mine_out)
    fetch_wait(sibs, sibs_out)
    fetch_wait(late.at[pl.ds(0, ROWS - 1)], late_out)
    fetch_wait(comb.at[pl.ds(0, len(BLOCKS) - 1)], comb_out)
    for b in range(BATCHES):
        if b in SUM_DIRECT:
            fetch_wait(part_in.at[b], part_out.at[b])
        else:
            fetch_wait(x_in.at[b], part_out.at[b])
            fetch_wait(y_in.at[b], y_out.at[b])
        fetch_wait(act.at[b, pl.ds(0, ROWS - 1)], act_out.at[b])
        fetch_wait(to_sib.at[b], fs_out.at[b])


PIECES = 2


def flush(x, gi, go, x_hbm, gi_hbm, go_hbm, sem):
    copies = [pltpu.make_async_copy(x, x_hbm, sem.at[2 * PIECES])]
    n = F // PIECES
    for i in range(PIECES):
        at = pl.ds(n * i, n)
        copies.append(pltpu.make_async_copy(gi.at[at], gi_hbm.at[at], sem.at[2 * i]))
        copies.append(pltpu.make_async_copy(go.at[at], go_hbm.at[at], sem.at[2 * i + 1]))
    for copy in copies:
        copy.start()
    for copy in copies:
        copy.wait()


def on_device(inputs, out_grad, w_in, w_out):
    vmem = pl.BlockSpec(memory_space=pltpu.VMEM)
    hbm = pl.BlockSpec(memory_space=pl.ANY)
    n = len(BLOCKS)
    dma = pltpu.SemaphoreType.DMA
    outs = pl.pallas_call(
        kernel,
        out_shape=(pltpu.VMEM((T, D), BF16), pltpu.VMEM((F, D), BF16), pltpu.VMEM((F, D), BF16)),
        in_specs=[hbm] * 4,
        out_specs=(vmem, vmem, vmem),
        scratch_shapes=[
            pltpu.VMEM((2, T, D), BF16),
            pltpu.VMEM((F, D), BF16),
            pltpu.VMEM((F, D), BF16),
            pltpu.VMEM((D, F), BF16),
            pltpu.VMEM((D, F), BF16),
            pltpu.VMEM((n, 2, 16, HALF), BF16),
            pltpu.VMEM((n, 2, 16, HALF), BF16),
            pltpu.VMEM((2, 16 * n, D), BF16),
            pltpu.VMEM((BATCHES, 4, 2, 16, F), BF16),
            pltpu.VMEM((BATCHES, ROWS - 1, 16, F), BF16),
            pltpu.VMEM((BATCHES, 3, 2, 16, F), BF16),
            pltpu.VMEM((BATCHES, 16, F), BF16),
            pltpu.VMEM((BATCHES, 16, F), BF16),
            pltpu.VMEM((BATCHES, 16, F), F32),
            pltpu.VMEM((BATCHES, ROWS, 16, WIDE), BF16),
            pltpu.VMEM((ROWS, BATCHES, 16, WIDE), BF16),
            pltpu.VMEM((16 * n, F), BF16),
            pltpu.VMEM((16 * n, F), BF16),
            pltpu.VMEM((BATCHES, PER, 16, HALF), BF16),
            pltpu.VMEM((BATCHES, PER, 16, HALF), F32),
            pltpu.VMEM((BATCHES, PER, 16, HALF), BF16),
            pltpu.VMEM((n, 16, HALF), BF16),
            pltpu.VMEM((n, 16, HALF), BF16),
            dma((2,)),
            dma((2,)),
            dma((n,)),
            dma((n,)),
            dma((BATCHES,)),
            dma((BATCHES,)),
            dma((BATCHES,)),
            dma((BATCHES,)),
            dma,
            dma,
            dma((BATCHES,)),
            dma((n,)),
            dma,
            dma,
            dma((BATCHES,)),
            dma((BATCHES,)),
            dma((BATCHES,)),
            dma,
            dma((BATCHES,)),
            dma,
        ],
        compiler_params=pltpu.CompilerParams(collective_id=0, has_side_effects=True, vmem_limit_bytes=44 << 20),
        name="block",
    )(*(pltpu.with_memory_space_constraint(a, pltpu.HBM) for a in (inputs, out_grad, w_in.T, w_out)))
    in_grad, w_in_grad, w_out_grad = pl.pallas_call(
        flush,
        out_shape=tuple(jax.ShapeDtypeStruct(o.shape, BF16) for o in outs),
        in_specs=[vmem] * 3,
        out_specs=(hbm,) * 3,
        scratch_shapes=[dma((2 * PIECES + 1,))],
        compiler_params=pltpu.CompilerParams(vmem_limit_bytes=16 << 20),
        name="flush",
    )(*outs)
    return (in_grad, w_in_grad.T, w_out_grad)


def solution(mesh):
    placed = (P("col", "row"), P("col", "row"), P("row", "col"), P("col", "row"))
    return jax.shard_map(
        on_device,
        mesh=mesh,
        in_specs=placed,
        out_specs=(P("col", "row"), P("row", "col"), P("col", "row")),
        check_vma=False,
    )
```

```python
import functools
import math

import jax
import jax.numpy as jnp
from jax import lax
from jax.experimental import pallas as pl
from jax.experimental.pallas import tpu as pltpu
from jax.sharding import PartitionSpec as P

MESH = pl.DeviceIdType.MESH
BF16, F32 = jnp.bfloat16, jnp.float32
NT = (((1,), (1,)), ((), ()))
NN = (((1,), (0,)), ((), ()))
TN = (((0,), (0,)), ((), ()))

T = 8
D = 1792
HALF = D // 2
F = 928
WIDE = 512
CUTS = (slice(0, WIDE), slice(WIDE, F))
ROWS = 8

BLOCKS = (
    (0, 2), (0, -2), (1, 0), (0, 1),
    (0, 4), (0, 3), (0, -3), (1, 2),
    (1, 4), (1, 3), (1, -3), (0, -1),
    (1, -2), (1, 1), (1, -1), (0, 0),
)
ONWARD = {
    (0, 0): ((0, 2), (0, -2), (1, 0), (0, 1), (0, -1)),
    (0, 2): ((1, 0), (0, -1)),
    (0, -2): ((1, 0), (0, 1)),
    (1, 0): ((0, 1), (0, -1)),
    (1, 2): ((0, -1),),
    (1, -2): ((0, 1),),
}
SLOT = {block: i for i, block in enumerate(BLOCKS)}
HOME = SLOT[(0, 0)]
BATCHES = 4
PER = len(BLOCKS) // BATCHES
TB = PER * 2 * T


def dot(a, b, dims):
    return lax.dot_general(a, b, dims, preferred_element_type=F32)


def mirrored(block):
    y, d = block
    return SLOT[(y, d if d == 4 else -d)]


def stack(a, b):
    return jnp.concatenate([a, b], axis=0)


def folded(low, high):
    pad = jnp.zeros((T, 2 * WIDE - F), F32)
    return stack(low, jnp.concatenate([high, pad], axis=1)).astype(BF16)


def unfold(ref, at, one, two):
    ref[at : at + 16, :WIDE] = stack(one[:T], two[:T])
    ref[at : at + 16, WIDE:] = stack(one[T:, : F - WIDE], two[T:, : F - WIDE])


def fetch_wait(ref, sem):
    pltpu.make_async_copy(ref, ref, sem).wait()


def kernel(
    x_in_hbm, x_og_hbm, w_in_hbm, w_out_hbm,
    in_grad, w_in_grad, w_out_grad,
    x, w_in, w_out, w_in_t, w_out_t, mine, sibs, acts, part_low, part_high, part_in_low, part_in_high, act, late, hid, pgr, to_sib, keep, from_sib, comb, comb_in,
    near_sem, far_sem, x_sem, w_sem, mine_sem, sibs_sem, part_sem, act_sem, late_sem, fs_sem, comb_sem,
    mine_out, sibs_out, part_out, act_out, late_out, fs_out, comb_out,
):
    parts, parts_in = (part_low, part_high), (part_in_low, part_in_high)
    r, c = lax.axis_index("row"), lax.axis_index("col")
    y_hi, z, k = c // 16, lax.rem(c // 2, 8), lax.rem(c, 2)

    def chip(y, d):
        return (r, lax.rem(y_hi + y, 2) * 16 + lax.rem(z + d + 8, 8) * 2 + k)

    sibling = (r, c + 1 - 2 * k)

    y_lo, x_at = r // 4, lax.rem(r, 4)
    me = 2 * x_at + y_lo
    y_peer = (lax.rem(r + 4, ROWS), c)

    def peer(j):
        return lax.rem(r + j, ROWS)

    def x_peer(j):
        return (4 * y_lo + lax.rem(x_at + j, 4), c)

    def send(src, dst, out, sem, to):
        pltpu.make_async_remote_copy(
            src_ref=src, dst_ref=dst, send_sem=out, recv_sem=sem, device_id=to, device_id_type=MESH
        ).start()

    weights = [pltpu.make_async_copy(w_in_hbm, w_in, w_sem.at[0]), pltpu.make_async_copy(w_out_hbm, w_out, w_sem.at[1])]
    tokens = [pltpu.make_async_copy(x_in_hbm, x.at[0], x_sem.at[0]), pltpu.make_async_copy(x_og_hbm, x.at[1], x_sem.at[1])]
    barrier = pltpu.get_barrier_semaphore()
    row_friends = [x_peer(1), x_peer(3), y_peer]
    friends = [chip(*block) for block in ONWARD[(0, 0)]] + [sibling] + row_friends
    for friend in friends:
        pl.semaphore_signal(barrier, inc=1, device_id=friend, device_id_type=MESH)
    for copy in tokens + weights:
        copy.start()
    for a in range(2):
        tokens[a].wait()
        block = x[a].astype(F32)
        mine[HOME, a] = stack(block[:, :HALF], block[:, HALF:]).astype(BF16)
    pl.semaphore_wait(barrier, len(friends))

    def forward(block):
        slot = SLOT[block]
        for to in ONWARD.get(block, ()):
            seen = SLOT[((block[0] + to[0]) % 2, block[1] - to[1])]
            send(mine.at[slot], mine.at[seen], mine_out, mine_sem.at[seen], chip(*to))
        if block[1] == -2:
            far, near = SLOT[(block[0], 4)], SLOT[(block[0], 2)]
            send(mine.at[near + k * (slot - near)], mine.at[far], mine_out, mine_sem.at[far], chip(0, 4 * k - 2))
        send(mine.at[slot], sibs.at[slot], sibs_out, sibs_sem.at[slot], sibling)

    def arrive(*blocks):
        for block in blocks:
            slot = SLOT[block]
            fetch_wait(mine.at[slot], mine_sem.at[slot])
            forward(block)

    def unpack(b):
        for s in range(PER * b, PER * b + PER):
            fetch_wait(sibs.at[s], sibs_sem.at[s])
            for a in range(2):
                own, sib = mine[s, a], sibs[s, a]
                acts[a, 16 * s : 16 * s + 16, :HALF] = stack(own[:T], sib[:T])
                acts[a, 16 * s : 16 * s + 16, HALF:] = stack(own[T:], sib[T:])

    def up(b, half):
        rows = slice(TB * b, TB * b + TB)
        pre = dot(acts[0, rows], w_in_t[:, CUTS[half]], NN)
        back = dot(acts[1, rows], w_out_t[:, CUTS[half]], NN)
        part, part_in, sem, out = parts[half], parts_in[half], part_sem.at[half, b], part_out.at[half, b]
        for i in range(ROWS):
            part[b, i // 2, i % 2] = stack(pre[T * i : T * i + T], back[T * i : T * i + T]).astype(BF16)
        for j in range(1, ROWS):
            to = peer(j)
            send(part.at[b, lax.rem(to, 4), to // 4], part_in.at[b, j - 1], out, sem, (to, c))

    def activate(b):
        hidden, grads = [], []
        for half in range(2):
            part, part_in = parts[half], parts_in[half]
            fetch_wait(part_in.at[b], part_sem.at[half, b])
            total = part[b, x_at, y_lo].astype(F32)
            for j in range(ROWS - 1):
                total += part_in[b, j].astype(F32)
            pre, back = total[:T], total[T:]
            cdf = 0.5 * (1.0 + lax.erf(pre * (1.0 / math.sqrt(2.0))))
            slope = cdf + pre * jnp.exp(-0.5 * pre * pre) * (1.0 / math.sqrt(2.0 * math.pi))
            hidden.append(pre * cdf)
            grads.append(back * slope)
        act[b, me] = folded(*grads)
        late[me, b] = folded(*hidden)
        own = act.at[b, me]
        for j in range(1, ROWS):
            send(own, own, act_out.at[b], act_sem.at[b], (peer(j), c))

    def spread_late():
        own = late.at[me]
        for j in range(1, ROWS):
            send(own, own, late_out, late_sem, (peer(j), c))

    def down(b):
        fetch_wait(act.at[b, pl.ds(0, ROWS - 1)], act_sem.at[b])
        for i in range(0, ROWS, 2):
            unfold(pgr, TB * b + T * i, act[b, i], act[b, i + 1])
        grad = dot(pgr[TB * b : TB * b + TB], w_in[...], NN)
        for i in range(PER):
            own, sib = grad[16 * i : 16 * i + T], grad[16 * i + T : 16 * i + 16]
            to_sib[b, i] = stack(sib[:, :HALF], sib[:, HALF:]).astype(BF16)
            keep[b, i] = stack(own[:, :HALF], own[:, HALF:])
        send(to_sib.at[b], from_sib.at[b], fs_out.at[b], fs_sem.at[b], sibling)

    def combine(b):
        fetch_wait(from_sib.at[b], fs_sem.at[b])
        for i in range(PER):
            s = PER * b + i
            total = keep[b, i] + from_sib[b, i].astype(F32)
            if s == HOME:
                keep[b, i] = total
            else:
                comb[s] = total.astype(BF16)
                seen = mirrored(BLOCKS[s])
                send(comb.at[s], comb_in.at[seen], comb_out, comb_sem.at[seen], chip(*BLOCKS[s]))

    forward((0, 0))
    for friend in row_friends:
        pl.semaphore_signal(near_sem, inc=1, device_id=friend, device_id_type=MESH)
    weights[0].wait()
    w_in_t[...] = w_in[...].T
    weights[1].wait()
    w_out_t[...] = w_out[...].T
    pl.semaphore_wait(near_sem, len(row_friends))
    pl.semaphore_signal(far_sem, inc=1, device_id=x_peer(1), device_id_type=MESH)
    arrive((0, 2), (0, -2), (1, 0), (0, 1), (0, -1))
    pl.semaphore_wait(far_sem, 1)
    unpack(0)
    up(0, 0)
    up(0, 1)
    arrive((0, 3), (0, -3), (1, 2), (1, -2), (0, 4), (1, 1), (1, -1))
    unpack(1)
    up(1, 0)
    up(1, 1)
    unpack(3)
    arrive((1, 3), (1, -3))
    up(3, 0)
    arrive((1, 4))
    up(3, 1)
    unpack(2)
    up(2, 0)
    up(2, 1)
    activate(0)
    activate(1)
    activate(2)
    down(0)
    activate(3)
    spread_late()
    combine(0)
    down(1)
    down(2)
    combine(1)
    combine(2)
    down(3)
    combine(3)
    w_in_grad[...] = dot(pgr[...], acts[0], TN).astype(BF16)
    fetch_wait(late.at[pl.ds(0, ROWS - 1)], late_sem)
    for b in range(BATCHES):
        for i in range(0, ROWS, 2):
            unfold(hid, TB * b + T * i, late[i, b], late[i + 1, b])
    w_out_grad[...] = dot(hid[...], acts[1], TN).astype(BF16)
    total = keep[HOME // PER, HOME % PER]
    for s in range(len(BLOCKS)):
        if s == HOME:
            continue
        fetch_wait(comb_in.at[s], comb_sem.at[s])
        total += comb_in[s].astype(F32)
    in_grad[:, :HALF] = total[:T].astype(BF16)
    in_grad[:, HALF:] = total[T:].astype(BF16)

    fetch_wait(mine.at[pl.ds(0, len(BLOCKS) - 1)], mine_out)
    fetch_wait(sibs, sibs_out)
    fetch_wait(late.at[pl.ds(0, ROWS - 1)], late_out)
    fetch_wait(comb.at[pl.ds(0, len(BLOCKS) - 1)], comb_out)
    for b in range(BATCHES):
        for half in range(2):
            fetch_wait(parts_in[half].at[b], part_out.at[half, b])
        fetch_wait(act.at[b, pl.ds(0, ROWS - 1)], act_out.at[b])
        fetch_wait(to_sib.at[b], fs_out.at[b])


PIECES = 2


def flush(x, gi, go, x_hbm, gi_hbm, go_hbm, sem):
    copies = [pltpu.make_async_copy(x, x_hbm, sem.at[2 * PIECES])]
    n = F // PIECES
    for i in range(PIECES):
        at = pl.ds(n * i, n)
        copies.append(pltpu.make_async_copy(gi.at[at], gi_hbm.at[at], sem.at[2 * i]))
        copies.append(pltpu.make_async_copy(go.at[at], go_hbm.at[at], sem.at[2 * i + 1]))
    for copy in copies:
        copy.start()
    for copy in copies:
        copy.wait()


def on_device(inputs, out_grad, w_in, w_out):
    vmem = pl.BlockSpec(memory_space=pltpu.VMEM)
    hbm = pl.BlockSpec(memory_space=pl.ANY)
    n = len(BLOCKS)
    dma = pltpu.SemaphoreType.DMA
    outs = pl.pallas_call(
        kernel,
        out_shape=(pltpu.VMEM((T, D), BF16), pltpu.VMEM((F, D), BF16), pltpu.VMEM((F, D), BF16)),
        in_specs=[hbm] * 4,
        out_specs=(vmem, vmem, vmem),
        scratch_shapes=[
            pltpu.VMEM((2, T, D), BF16),
            pltpu.VMEM((F, D), BF16),
            pltpu.VMEM((F, D), BF16),
            pltpu.VMEM((D, F), BF16),
            pltpu.VMEM((D, F), BF16),
            pltpu.VMEM((n, 2, 16, HALF), BF16),
            pltpu.VMEM((n, 2, 16, HALF), BF16),
            pltpu.VMEM((2, 16 * n, D), BF16),
            pltpu.VMEM((BATCHES, 4, 2, 16, WIDE), BF16),
            pltpu.VMEM((BATCHES, 4, 2, 16, F - WIDE), BF16),
            pltpu.VMEM((BATCHES, ROWS - 1, 16, WIDE), BF16),
            pltpu.VMEM((BATCHES, ROWS - 1, 16, F - WIDE), BF16),
            pltpu.VMEM((BATCHES, ROWS, 16, WIDE), BF16),
            pltpu.VMEM((ROWS, BATCHES, 16, WIDE), BF16),
            pltpu.VMEM((16 * n, F), BF16),
            pltpu.VMEM((16 * n, F), BF16),
            pltpu.VMEM((BATCHES, PER, 16, HALF), BF16),
            pltpu.VMEM((BATCHES, PER, 16, HALF), F32),
            pltpu.VMEM((BATCHES, PER, 16, HALF), BF16),
            pltpu.VMEM((n, 16, HALF), BF16),
            pltpu.VMEM((n, 16, HALF), BF16),
            pltpu.SemaphoreType.REGULAR,
            pltpu.SemaphoreType.REGULAR,
            dma((2,)),
            dma((2,)),
            dma((n,)),
            dma((n,)),
            dma((2, BATCHES)),
            dma((BATCHES,)),
            dma,
            dma((BATCHES,)),
            dma((n,)),
            dma,
            dma,
            dma((2, BATCHES)),
            dma((BATCHES,)),
            dma,
            dma((BATCHES,)),
            dma,
        ],
        compiler_params=pltpu.CompilerParams(collective_id=0, has_side_effects=True, vmem_limit_bytes=44 << 20),
        name="block",
    )(*(pltpu.with_memory_space_constraint(a, pltpu.HBM) for a in (inputs, out_grad, w_in.T, w_out)))
    in_grad, w_in_grad, w_out_grad = pl.pallas_call(
        flush,
        out_shape=tuple(jax.ShapeDtypeStruct(o.shape, BF16) for o in outs),
        in_specs=[vmem] * 3,
        out_specs=(hbm,) * 3,
        scratch_shapes=[dma((2 * PIECES + 1,))],
        compiler_params=pltpu.CompilerParams(vmem_limit_bytes=16 << 20),
        name="flush",
    )(*outs)
    return (in_grad, w_in_grad.T, w_out_grad)


def solution(mesh):
    placed = (P("col", "row"), P("col", "row"), P("row", "col"), P("col", "row"))
    return jax.shard_map(
        on_device,
        mesh=mesh,
        in_specs=placed,
        out_specs=(P("col", "row"), P("row", "col"), P("col", "row")),
        check_vma=False,
    )
```

```python
import functools
import math

import jax
import jax.numpy as jnp
from jax import lax
from jax.experimental import pallas as pl
from jax.experimental.pallas import tpu as pltpu
from jax.sharding import PartitionSpec as P

MESH = pl.DeviceIdType.MESH
BF16, F32 = jnp.bfloat16, jnp.float32
NT = (((1,), (1,)), ((), ()))
NN = (((1,), (0,)), ((), ()))
TN = (((0,), (0,)), ((), ()))

T = 8
D = 1792
HALF = D // 2
F = 928
WIDE = 512
CUTS = (slice(0, WIDE), slice(WIDE, F))
ROWS = 8

BLOCKS = (
    (0, 2), (0, -2), (1, 0), (0, 1),
    (0, 4), (0, 3), (0, -3), (1, 2),
    (1, 4), (1, 3), (1, -3), (0, -1),
    (1, -2), (1, 1), (1, -1), (0, 0),
)
ONWARD = {
    (0, 0): ((0, 2), (0, -2), (1, 0), (0, 1), (0, -1)),
    (0, 2): ((1, 0), (0, -1)),
    (0, -2): ((1, 0), (0, 1)),
    (1, 0): ((0, 1), (0, -1)),
    (1, 2): ((0, -1),),
    (1, -2): ((0, 1),),
}
SLOT = {block: i for i, block in enumerate(BLOCKS)}
HOME = SLOT[(0, 0)]
BATCHES = 4
PER = len(BLOCKS) // BATCHES
TB = PER * 2 * T


def dot(a, b, dims):
    return lax.dot_general(a, b, dims, preferred_element_type=F32)


def mirrored(block):
    y, d = block
    return SLOT[(y, d if d == 4 else -d)]


def stack(a, b):
    return jnp.concatenate([a, b], axis=0)


def folded(low, high):
    pad = jnp.zeros((T, 2 * WIDE - F), F32)
    return stack(low, jnp.concatenate([high, pad], axis=1)).astype(BF16)


def unfold(ref, at, one, two):
    ref[at : at + 16, :WIDE] = stack(one[:T], two[:T])
    ref[at : at + 16, WIDE:] = stack(one[T:, : F - WIDE], two[T:, : F - WIDE])


def fetch_wait(ref, sem):
    pltpu.make_async_copy(ref, ref, sem).wait()


def kernel(
    x_in_hbm, x_og_hbm, w_in_hbm, w_out_hbm,
    in_grad, w_in_grad, w_out_grad,
    x, w_in, w_out, w_in_t, w_out_t, mine, sibs, acts, part_low, part_high, part_in_low, part_in_high, act, late, hid, pgr, to_sib, keep, from_sib, comb, comb_in,
    near_sem, far_sem, x_sem, w_sem, mine_sem, sibs_sem, part_sem, act_sem, late_sem, fs_sem, comb_sem,
    mine_out, sibs_out, part_out, act_out, late_out, fs_out, comb_out,
):
    parts, parts_in = (part_low, part_high), (part_in_low, part_in_high)
    r, c = lax.axis_index("row"), lax.axis_index("col")
    y_hi, z, k = c // 16, lax.rem(c // 2, 8), lax.rem(c, 2)

    def chip(y, d):
        return (r, lax.rem(y_hi + y, 2) * 16 + lax.rem(z + d + 8, 8) * 2 + k)

    sibling = (r, c + 1 - 2 * k)

    y_lo, x_at = r // 4, lax.rem(r, 4)
    me = 2 * x_at + y_lo
    y_peer = (lax.rem(r + 4, ROWS), c)

    def peer(j):
        return lax.rem(r + j, ROWS)

    def x_peer(j):
        return (4 * y_lo + lax.rem(x_at + j, 4), c)

    def send(src, dst, out, sem, to):
        pltpu.make_async_remote_copy(
            src_ref=src, dst_ref=dst, send_sem=out, recv_sem=sem, device_id=to, device_id_type=MESH
        ).start()

    weights = [pltpu.make_async_copy(w_in_hbm, w_in, w_sem.at[0]), pltpu.make_async_copy(w_out_hbm, w_out, w_sem.at[1])]
    tokens = [pltpu.make_async_copy(x_in_hbm, x.at[0], x_sem.at[0]), pltpu.make_async_copy(x_og_hbm, x.at[1], x_sem.at[1])]
    barrier = pltpu.get_barrier_semaphore()
    row_friends = [x_peer(1), x_peer(3), y_peer]
    friends = [chip(*block) for block in ONWARD[(0, 0)]] + [sibling] + row_friends
    for friend in friends:
        pl.semaphore_signal(barrier, inc=1, device_id=friend, device_id_type=MESH)
    for copy in tokens:
        copy.start()
    for a in range(2):
        tokens[a].wait()
        block = x[a].astype(F32)
        mine[HOME, a] = stack(block[:, :HALF], block[:, HALF:]).astype(BF16)
    for copy in weights:
        copy.start()
    pl.semaphore_wait(barrier, len(friends))

    def forward(block):
        slot = SLOT[block]
        for to in ONWARD.get(block, ()):
            seen = SLOT[((block[0] + to[0]) % 2, block[1] - to[1])]
            send(mine.at[slot], mine.at[seen], mine_out, mine_sem.at[seen], chip(*to))
        if block[1] == -2:
            far, near = SLOT[(block[0], 4)], SLOT[(block[0], 2)]
            send(mine.at[near + k * (slot - near)], mine.at[far], mine_out, mine_sem.at[far], chip(0, 4 * k - 2))
        send(mine.at[slot], sibs.at[slot], sibs_out, sibs_sem.at[slot], sibling)

    def arrive(*blocks):
        for block in blocks:
            slot = SLOT[block]
            fetch_wait(mine.at[slot], mine_sem.at[slot])
            forward(block)

    def unpack(b):
        for s in range(PER * b, PER * b + PER):
            fetch_wait(sibs.at[s], sibs_sem.at[s])
            for a in range(2):
                own, sib = mine[s, a], sibs[s, a]
                acts[a, 16 * s : 16 * s + 16, :HALF] = stack(own[:T], sib[:T])
                acts[a, 16 * s : 16 * s + 16, HALF:] = stack(own[T:], sib[T:])

    def up(b, half):
        rows = slice(TB * b, TB * b + TB)
        pre = dot(acts[0, rows], w_in_t[:, CUTS[half]], NN)
        back = dot(acts[1, rows], w_out_t[:, CUTS[half]], NN)
        part, part_in, sem, out = parts[half], parts_in[half], part_sem.at[half, b], part_out.at[half, b]
        for i in range(ROWS):
            part[b, i // 2, i % 2] = stack(pre[T * i : T * i + T], back[T * i : T * i + T]).astype(BF16)
        for j in range(1, ROWS):
            to = peer(j)
            send(part.at[b, lax.rem(to, 4), to // 4], part_in.at[b, j - 1], out, sem, (to, c))

    def activate(b):
        hidden, grads = [], []
        for half in range(2):
            part, part_in = parts[half], parts_in[half]
            fetch_wait(part_in.at[b], part_sem.at[half, b])
            total = part[b, x_at, y_lo].astype(F32)
            for j in range(ROWS - 1):
                total += part_in[b, j].astype(F32)
            pre, back = total[:T], total[T:]
            cdf = 0.5 * (1.0 + lax.erf(pre * (1.0 / math.sqrt(2.0))))
            slope = cdf + pre * jnp.exp(-0.5 * pre * pre) * (1.0 / math.sqrt(2.0 * math.pi))
            hidden.append(pre * cdf)
            grads.append(back * slope)
        act[b, me] = folded(*grads)
        late[me, b] = folded(*hidden)
        own = act.at[b, me]
        for j in range(1, ROWS):
            send(own, own, act_out.at[b], act_sem.at[b], (peer(j), c))

    def spread_late():
        own = late.at[me]
        for j in range(1, ROWS):
            send(own, own, late_out, late_sem, (peer(j), c))

    def down(b):
        fetch_wait(act.at[b, pl.ds(0, ROWS - 1)], act_sem.at[b])
        for i in range(0, ROWS, 2):
            unfold(pgr, TB * b + T * i, act[b, i], act[b, i + 1])
        grad = dot(pgr[TB * b : TB * b + TB], w_in[...], NN)
        for i in range(PER):
            own, sib = grad[16 * i : 16 * i + T], grad[16 * i + T : 16 * i + 16]
            to_sib[b, i] = stack(sib[:, :HALF], sib[:, HALF:]).astype(BF16)
            keep[b, i] = stack(own[:, :HALF], own[:, HALF:])
        send(to_sib.at[b], from_sib.at[b], fs_out.at[b], fs_sem.at[b], sibling)

    def combine(b):
        fetch_wait(from_sib.at[b], fs_sem.at[b])
        for i in range(PER):
            s = PER * b + i
            total = keep[b, i] + from_sib[b, i].astype(F32)
            if s == HOME:
                keep[b, i] = total
            else:
                comb[s] = total.astype(BF16)
                seen = mirrored(BLOCKS[s])
                send(comb.at[s], comb_in.at[seen], comb_out, comb_sem.at[seen], chip(*BLOCKS[s]))

    forward((0, 0))
    for friend in row_friends:
        pl.semaphore_signal(near_sem, inc=1, device_id=friend, device_id_type=MESH)
    weights[0].wait()
    w_in_t[...] = w_in[...].T
    weights[1].wait()
    w_out_t[...] = w_out[...].T
    pl.semaphore_wait(near_sem, len(row_friends))
    pl.semaphore_signal(far_sem, inc=1, device_id=x_peer(1), device_id_type=MESH)
    arrive((0, 2), (0, -2), (1, 0), (0, 1), (0, -1))
    pl.semaphore_wait(far_sem, 1)
    unpack(0)
    up(0, 0)
    up(0, 1)
    arrive((0, 3), (0, -3), (1, 2), (1, -2), (0, 4), (1, 1), (1, -1))
    unpack(1)
    up(1, 0)
    up(1, 1)
    unpack(3)
    arrive((1, 3), (1, -3))
    up(3, 0)
    arrive((1, 4))
    up(3, 1)
    unpack(2)
    up(2, 0)
    up(2, 1)
    activate(0)
    activate(1)
    activate(3)
    down(0)
    activate(2)
    spread_late()
    combine(0)
    down(1)
    down(3)
    combine(1)
    combine(3)
    down(2)
    combine(2)
    w_in_grad[...] = dot(pgr[...], acts[0], TN).astype(BF16)
    fetch_wait(late.at[pl.ds(0, ROWS - 1)], late_sem)
    for b in range(BATCHES):
        for i in range(0, ROWS, 2):
            unfold(hid, TB * b + T * i, late[i, b], late[i + 1, b])
    w_out_grad[...] = dot(hid[...], acts[1], TN).astype(BF16)
    total = keep[HOME // PER, HOME % PER]
    for s in range(len(BLOCKS)):
        if s == HOME:
            continue
        fetch_wait(comb_in.at[s], comb_sem.at[s])
        total += comb_in[s].astype(F32)
    in_grad[:, :HALF] = total[:T].astype(BF16)
    in_grad[:, HALF:] = total[T:].astype(BF16)

    fetch_wait(mine.at[pl.ds(0, len(BLOCKS) - 1)], mine_out)
    fetch_wait(sibs, sibs_out)
    fetch_wait(late.at[pl.ds(0, ROWS - 1)], late_out)
    fetch_wait(comb.at[pl.ds(0, len(BLOCKS) - 1)], comb_out)
    for b in range(BATCHES):
        for half in range(2):
            fetch_wait(parts_in[half].at[b], part_out.at[half, b])
        fetch_wait(act.at[b, pl.ds(0, ROWS - 1)], act_out.at[b])
        fetch_wait(to_sib.at[b], fs_out.at[b])


PIECES = 2


def flush(x, gi, go, x_hbm, gi_hbm, go_hbm, sem):
    copies = [pltpu.make_async_copy(x, x_hbm, sem.at[2 * PIECES])]
    n = F // PIECES
    for i in range(PIECES):
        at = pl.ds(n * i, n)
        copies.append(pltpu.make_async_copy(gi.at[at], gi_hbm.at[at], sem.at[2 * i]))
        copies.append(pltpu.make_async_copy(go.at[at], go_hbm.at[at], sem.at[2 * i + 1]))
    for copy in copies:
        copy.start()
    for copy in copies:
        copy.wait()


def on_device(inputs, out_grad, w_in, w_out):
    vmem = pl.BlockSpec(memory_space=pltpu.VMEM)
    hbm = pl.BlockSpec(memory_space=pl.ANY)
    n = len(BLOCKS)
    dma = pltpu.SemaphoreType.DMA
    outs = pl.pallas_call(
        kernel,
        out_shape=(pltpu.VMEM((T, D), BF16), pltpu.VMEM((F, D), BF16), pltpu.VMEM((F, D), BF16)),
        in_specs=[hbm] * 4,
        out_specs=(vmem, vmem, vmem),
        scratch_shapes=[
            pltpu.VMEM((2, T, D), BF16),
            pltpu.VMEM((F, D), BF16),
            pltpu.VMEM((F, D), BF16),
            pltpu.VMEM((D, F), BF16),
            pltpu.VMEM((D, F), BF16),
            pltpu.VMEM((n, 2, 16, HALF), BF16),
            pltpu.VMEM((n, 2, 16, HALF), BF16),
            pltpu.VMEM((2, 16 * n, D), BF16),
            pltpu.VMEM((BATCHES, 4, 2, 16, WIDE), BF16),
            pltpu.VMEM((BATCHES, 4, 2, 16, F - WIDE), BF16),
            pltpu.VMEM((BATCHES, ROWS - 1, 16, WIDE), BF16),
            pltpu.VMEM((BATCHES, ROWS - 1, 16, F - WIDE), BF16),
            pltpu.VMEM((BATCHES, ROWS, 16, WIDE), BF16),
            pltpu.VMEM((ROWS, BATCHES, 16, WIDE), BF16),
            pltpu.VMEM((16 * n, F), BF16),
            pltpu.VMEM((16 * n, F), BF16),
            pltpu.VMEM((BATCHES, PER, 16, HALF), BF16),
            pltpu.VMEM((BATCHES, PER, 16, HALF), F32),
            pltpu.VMEM((BATCHES, PER, 16, HALF), BF16),
            pltpu.VMEM((n, 16, HALF), BF16),
            pltpu.VMEM((n, 16, HALF), BF16),
            pltpu.SemaphoreType.REGULAR,
            pltpu.SemaphoreType.REGULAR,
            dma((2,)),
            dma((2,)),
            dma((n,)),
            dma((n,)),
            dma((2, BATCHES)),
            dma((BATCHES,)),
            dma,
            dma((BATCHES,)),
            dma((n,)),
            dma,
            dma,
            dma((2, BATCHES)),
            dma((BATCHES,)),
            dma,
            dma((BATCHES,)),
            dma,
        ],
        compiler_params=pltpu.CompilerParams(collective_id=0, has_side_effects=True, vmem_limit_bytes=44 << 20),
        name="block",
    )(*(pltpu.with_memory_space_constraint(a, pltpu.HBM) for a in (inputs, out_grad, w_in.T, w_out)))
    in_grad, w_in_grad, w_out_grad = pl.pallas_call(
        flush,
        out_shape=tuple(jax.ShapeDtypeStruct(o.shape, BF16) for o in outs),
        in_specs=[vmem] * 3,
        out_specs=(hbm,) * 3,
        scratch_shapes=[dma((2 * PIECES + 1,))],
        compiler_params=pltpu.CompilerParams(vmem_limit_bytes=16 << 20),
        name="flush",
    )(*outs)
    return (in_grad, w_in_grad.T, w_out_grad)


def solution(mesh):
    placed = (P("col", "row"), P("col", "row"), P("row", "col"), P("col", "row"))
    return jax.shard_map(
        on_device,
        mesh=mesh,
        in_specs=placed,
        out_specs=(P("col", "row"), P("row", "col"), P("col", "row")),
        check_vma=False,
    )
```
